512 devices in a mesh: row: 32 (over y, x, core), col: 16 (over z).
Axes of the slice: x: 4, y: 4, z: 16, core: 2. Of those that a mesh axis runs over, the one named last changes fastest.
Arguments:
- x_start: bfloat16 [64, 131072], P(None, ('row', 'col')), may hold values from -6 to 6
- weights: float32 [131072], P(('row', 'col')), may hold values from 1 to 10
- blocks: bfloat16 [4608, 512, 512], P(('row', 'col')), may hold values from -0.25 to 0.25
- block_rows: int32 [4608], P(('row', 'col')), may hold values from 0 to 7
- block_cols: int32 [4608], P(('row', 'col')), may hold values from 0 to 15
- live_blocks: int32 [512], P(('row', 'col')), may hold values from 1 to 9, as said below
Outputs:
- embedding: bfloat16 [64, 131072], P(None, ('row', 'col'))
The draws below stay inside these ranges and needn't reach their ends.
Inputs may be any that keep to these rules, and one draw needn't show every extreme that they name: `live_blocks`: some cell has all 9 slots live.
All inputs are finite; a program needn't handle non-finite values.
Results may differ from the reference program's by a relative error of at most 0.023.
Values may be sent and summed in bfloat16 or wider, within the bound.
No kernel may reach another device: no remote copies, remote signals or barrier semaphores. Data moves between devices by JAX's collectives and lax.ppermute only.
A program may use at most 64 MiB of HBM per device.

```python
import jax
import jax.numpy as jnp
from jax import lax

K = 64
TILE = 512
RDEV = 256
NBLK = 9
ITERS = 2
NV = 131072
RLEN = 4096
CLEN = 8192
RBLK = 8
CBLK = 16
SLOTS = 4608
N_ROW = 32
N_COL = 16
DEVICES = 512


def draw_weights(key, part):
    key = jax.random.fold_in(key, 11)
    position = jnp.arange(NV, dtype=jnp.float32) / NV
    noise = jax.random.uniform(key, (NV,), jnp.float32)
    mixed = 0.5 * position + 0.5 * noise
    return jnp.exp(jnp.log(10.0) * mixed).astype(jnp.float32)


def draw_live_blocks(key, part):
    key = jax.random.fold_in(key, 5)
    first_key, second_key, third_key = jax.random.split(key, 3)
    first_draw = jax.random.randint(first_key, (DEVICES,), 0, NBLK)
    second_draw = jax.random.randint(second_key, (DEVICES,), 0, NBLK)
    busiest = jax.random.randint(third_key, (), 0, DEVICES)
    counts = jnp.minimum(first_draw, second_draw) + 1
    return jnp.where(jnp.arange(DEVICES) == busiest, NBLK, counts).astype(jnp.int32)


def place_ends(entries, rng, low, top_value):
    longest = entries.shape.index(max(entries.shape))
    spots = []
    for shift in (0, 1):
        where = [jax.random.randint(jax.random.fold_in(rng, axis), (), 0, length) for axis, length in enumerate(entries.shape)]
        where[longest] = (where[longest] + shift) % entries.shape[longest]
        spots.append(tuple(where))
    return entries.at[spots[0]].set(low).at[spots[1]].set(top_value)


def level_of(key, dims, cuts, low, high):
    factor_of = 1.0
    for dim, shards_of in cuts:
        heights = jax.random.uniform(jax.random.fold_in(jax.random.fold_in(key, 6), dim), (shards_of,), jnp.float32, low / len(cuts), high / len(cuts))
        factor_of = factor_of * jnp.repeat(jnp.exp(heights), dims[dim] // shards_of).reshape((-1,) + (1,) * (len(dims) - 1 - dim))
    return factor_of


def bell_draw(rng, dims, spread, limit, cuts=(), kind=jnp.bfloat16):
    gain = level_of(rng, dims, cuts, -0.22, 0.18) if cuts else 1.0
    values = jax.random.normal(rng, dims, jnp.float32) * spread * gain
    return jnp.minimum(jnp.maximum(values, -limit), limit).astype(kind)


def setup_inputs(seed: int = 0) -> dict:
    arg_keys = jax.random.split(jax.random.key(seed), 7)
    return {
        "x_start": bell_draw(arg_keys[0], (K, NV), 1.0, 6.0, ((1, 512),)),
        "weights": draw_weights(jax.random.fold_in(arg_keys[6], 71), 0),
        "blocks": bell_draw(arg_keys[2], (SLOTS, TILE, TILE), TILE ** -0.5, 0.25, ((0, 512),)),
        "block_rows": place_ends(jax.random.randint(arg_keys[3], (SLOTS,), 0, RBLK), jax.random.fold_in(arg_keys[3], 1), 0, RBLK - 1).astype(jnp.int32),
        "block_cols": place_ends(jax.random.randint(arg_keys[4], (SLOTS,), 0, CBLK), jax.random.fold_in(arg_keys[4], 1), 0, CBLK - 1).astype(jnp.int32),
        "live_blocks": draw_live_blocks(jax.random.fold_in(arg_keys[6], 71), 0),
    }


def cell_terms(row_panel, col_panel, cell_tiles, cell_rows, cell_cols, live_count):
    vector_count = row_panel.shape[0]
    live_mask = (jnp.arange(NBLK, dtype=jnp.int32) < live_count).astype(jnp.float32)
    row_tiles = row_panel.reshape(vector_count, RBLK, TILE)
    col_tiles = col_panel.reshape(vector_count, CBLK, TILE)
    picked_cols = jnp.take(col_tiles, cell_cols, axis=1).astype(jnp.float32)
    picked_rows = jnp.take(row_tiles, cell_rows, axis=1).astype(jnp.float32)
    tiles_wide = cell_tiles.astype(jnp.float32)
    direct = jnp.einsum('ksj,sij->ksi', picked_cols, tiles_wide, precision=lax.Precision.HIGHEST)
    mirror = jnp.einsum('ksi,sij->ksj', picked_rows, tiles_wide, precision=lax.Precision.HIGHEST)
    row_hot = (cell_rows[:, None] == jnp.arange(RBLK, dtype=jnp.int32)[None, :]).astype(jnp.float32) * live_mask[:, None]
    col_hot = (cell_cols[:, None] == jnp.arange(CBLK, dtype=jnp.int32)[None, :]).astype(jnp.float32) * live_mask[:, None]
    direct_sum = jnp.einsum('sa,ksi->kai', row_hot, direct, precision=lax.Precision.HIGHEST).reshape(vector_count, RLEN)
    mirror_sum = jnp.einsum('sb,ksj->kbj', col_hot, mirror, precision=lax.Precision.HIGHEST).reshape(vector_count, CLEN)
    return (direct_sum.astype(jnp.bfloat16), mirror_sum.astype(jnp.bfloat16))

def reference(x_start, weights, blocks, block_rows, block_cols, live_blocks):
    vector_count = x_start.shape[0]
    tiles_all = blocks.reshape(DEVICES, NBLK, TILE, TILE)
    rows_all = block_rows.reshape(DEVICES, NBLK)
    cols_all = block_cols.reshape(DEVICES, NBLK)
    cell_ids = jnp.arange(DEVICES, dtype=jnp.int32)
    identity = jnp.eye(vector_count, dtype=jnp.float32)
    current = x_start
    for sweep_index in range(ITERS):
        scaled = (current.astype(jnp.float32) * weights[None, :]).astype(jnp.bfloat16)
        vertex_grid = scaled.reshape(vector_count, N_ROW, N_COL, RDEV)

        def one_cell(cell_items):
            cell_index, cell_tiles, cell_rows, cell_cols, live_count = cell_items
            row_panel = lax.dynamic_index_in_dim(vertex_grid, cell_index // N_COL, 1, keepdims=False).reshape(vector_count, RLEN)
            col_panel = lax.dynamic_index_in_dim(vertex_grid, cell_index % N_COL, 2, keepdims=False).reshape(vector_count, CLEN)
            return cell_terms(row_panel, col_panel, cell_tiles, cell_rows, cell_cols, live_count)
        direct, mirror = lax.map(one_cell, (cell_ids, tiles_all, rows_all, cols_all, live_blocks))
        direct_total = jnp.sum(direct.astype(jnp.float32).reshape(N_ROW, N_COL, vector_count, N_COL, RDEV), axis=1)
        direct_total = jnp.transpose(direct_total, (1, 0, 2, 3)).reshape(vector_count, NV)
        mirror_total = jnp.sum(mirror.astype(jnp.float32).reshape(N_ROW, N_COL, vector_count, N_ROW, RDEV), axis=0)
        mirror_total = jnp.transpose(mirror_total, (1, 2, 0, 3)).reshape(vector_count, NV)
        fresh_panel = ((direct_total + mirror_total) * weights[None, :]).astype(jnp.bfloat16)
        gram_matrix = lax.dot_general(fresh_panel.astype(jnp.float32), fresh_panel.astype(jnp.float32), (((1,), (1,)), ((), ())), preferred_element_type=jnp.float32) / NV + 1e-06 * identity
        lower_factor = jnp.linalg.cholesky(gram_matrix)
        lower_inverse = lax.linalg.triangular_solve(lower_factor, identity, left_side=True, lower=True)
        current = jnp.dot(lower_inverse, fresh_panel.astype(jnp.float32), precision=lax.Precision.HIGHEST).astype(jnp.bfloat16)
    return current
```

```python
import functools

import jax
import jax.numpy as jnp
from jax import lax
from jax.experimental import pallas as pl
from jax.experimental.pallas import tpu as pltpu
from jax.sharding import Mesh, PartitionSpec as P

F32 = jnp.float32
BF16 = jnp.bfloat16
ROW = ("y", "x", "core")
RIDGE = 1e-06
VMEM = pl.BlockSpec(memory_space=pltpu.VMEM)
SMEM = pl.BlockSpec(memory_space=pltpu.SMEM)
PARAMS = pltpu.CompilerParams(vmem_limit_bytes=48 * 1024 * 1024)
NT = (((1,), (1,)), ((), ()))
NN = (((1,), (0,)), ((), ()))


def call(kernel, outs, ins, scratch=(), flops=0, moved=0):
    return pl.pallas_call(
        kernel,
        out_shape=[jax.ShapeDtypeStruct(s, d) for s, d in outs],
        in_specs=ins,
        out_specs=[VMEM] * len(outs),
        scratch_shapes=list(scratch),
        compiler_params=PARAMS,
        cost_estimate=pl.CostEstimate(flops=flops, bytes_accessed=moved, transcendentals=0),
    )


def start_tiles(blocks, held, sems):
    slots = held.shape[0]
    copies = [pltpu.make_async_copy(blocks.at[s], held.at[s], sems.at[s]) for s in range(slots)]
    for copy in copies:
        copy.start()
    return copies


def direct_kernel(rows, cols, live, panel, blocks, out, held, total, sems):
    copies = start_tiles(blocks, held, sems)
    total[...] = jnp.zeros_like(total)
    half = panel.shape[2]
    for s, copy in enumerate(copies):
        copy.wait()

        @pl.when(s < live[0])
        def _():
            r, c = rows[s], cols[s]
            part = lax.dot_general(
                panel[2 * c], held[s, :, :half], NT, preferred_element_type=F32
            ) + lax.dot_general(panel[2 * c + 1], held[s, :, half:], NT, preferred_element_type=F32)
            total[2 * r] += part[:, :half]
            total[2 * r + 1] += part[:, half:]

    out[...] = total[...].astype(BF16)


def mirror_kernel(rows, cols, live, panel, blocks, keep, send, held, total, sems):
    copies = start_tiles(blocks, held, sems)
    total[...] = jnp.zeros_like(total)
    half = panel.shape[2]
    for s, copy in enumerate(copies):
        copy.wait()

        @pl.when(s < live[0])
        def _():
            r, c = rows[s], cols[s]
            part = lax.dot_general(
                panel[2 * r], held[s, :half, :], NN, preferred_element_type=F32
            ) + lax.dot_general(panel[2 * r + 1], held[s, half:, :], NN, preferred_element_type=F32)
            total[2 * c] += part[:, :half]
            total[2 * c + 1] += part[:, half:]

    me = lax.axis_index("core")
    for chip in range(keep.shape[0]):
        keep[chip] = total[2 * chip + me].astype(BF16)
        send[chip] = total[2 * chip + 1 - me].astype(BF16)


def merge_x_kernel(keep, got, *pieces):
    me = lax.axis_index("x")
    n = len(pieces)
    for k, piece in enumerate(pieces):
        to = lax.rem(me + k, n)
        for y in range(piece.shape[0]):
            piece[y] = (keep[y * n + to].astype(F32) + got[y * n + to].astype(F32)).astype(BF16)


def merge_y_kernel(own, *refs):
    n = own.shape[0]
    got, pieces = refs[: n - 1], refs[n - 1 :]
    me = lax.axis_index("y")
    for k, piece in enumerate(pieces):
        to = lax.rem(me + k, n)
        sums = own[to].astype(F32)
        for g in got:
            sums += g[to].astype(F32)
        piece[...] = sums.astype(BF16)


def spread(value, scaled, copies):
    scaled[...] = value
    for k in range(copies.shape[0]):
        copies[k] = value


def prepare_kernel(x, weights, scaled, copies):
    spread((x[...].astype(F32) * weights[...]).astype(BF16), scaled, copies)


def add_up(arrived, own, others, weights):
    sums = own[...].astype(F32)
    for other in others:
        sums += other[...].astype(F32)
    for k in range(arrived.shape[0]):
        sums += arrived[k].astype(F32)
    return sums * weights[...]


def between_kernel(arrived, weights, own, s1, s2, s3, scaled, copies, gram):
    fresh = add_up(arrived, own, (s1, s2, s3), weights)
    spread((fresh * weights[...]).astype(BF16), scaled, copies)
    rounded = fresh.astype(BF16)
    gram[...] = lax.dot_general(rounded, rounded, NT, preferred_element_type=F32)


def fold(matrix):
    h = matrix.shape[0] // 2
    return jnp.concatenate([matrix[:h], matrix[h:]], axis=1)


def last_kernel(scale, arrived, weights, own, s1, s2, s3, first, fresh, keep, send):
    rounded = add_up(arrived, own, (s1, s2, s3), weights).astype(BF16)
    fresh[...] = rounded
    gram = lax.dot_general(rounded, rounded, NT, preferred_element_type=F32)
    gram = (gram + RIDGE * first[...]) * scale
    h = gram.shape[0] // 2
    low, high = fold(gram[:h]), fold(gram[h:])
    second = lax.axis_index("core") == 1
    keep[...] = jnp.where(second, high, low)
    send[...] = jnp.where(second, low, high)


def whiten_kernel(parts, fresh, out, factor):
    n = fresh.shape[0]
    halves = [parts[0], parts[1]]
    matrix = jnp.concatenate([p for h in halves for p in (h[:, :n], h[:, n:])], axis=0)
    eye = (
        lax.broadcasted_iota(jnp.int32, (n, n), 0) == lax.broadcasted_iota(jnp.int32, (n, n), 1)
    ).astype(F32)
    left = jnp.concatenate([matrix + RIDGE * RIDGE * eye, eye], axis=1)
    base = 0
    for j in range(0, n, 2):
        if j - base == 8:
            left = left[8:]
            base = j
        i = j - base
        row0, row1 = left[i : i + 1], left[i + 1 : i + 2]
        col0, col1 = left[:, j : j + 1], left[:, j + 1 : j + 2]
        p0, q = row0[:, j : j + 1], row0[:, j + 1 : j + 2]
        inv0 = 1.0 / p0
        t = q * inv0
        p1 = row1[:, j + 1 : j + 2] - q * t
        inv1 = 1.0 / p1
        row1 = row1 - t * row0
        col1 = col1 - t * col0
        factor[j : j + 1] = row0 * (1.0 / jnp.sqrt(p0))
        factor[j + 1 : j + 2] = row1 * (1.0 / jnp.sqrt(p1))
        left = left - (col0 * inv0) * row0 - (col1 * inv1) * row1
    inverse = factor[:, n:]
    out[...] = lax.dot_general(
        inverse,
        fresh[...].astype(F32),
        NN,
        precision=lax.Precision.HIGHEST,
        preferred_element_type=F32,
    ).astype(BF16)


def swap(value, axis, shift, size):
    return lax.ppermute(value, axis, [(i, (i + shift) % size) for i in range(size)])


def exchange(value, axes):
    return lax.all_to_all(value, axes, split_axis=0, concat_axis=0, tiled=True)


def body(x_start, weights, blocks, block_rows, block_cols, live_blocks):
    k, own = x_start.shape
    slots, tile, _ = blocks.shape
    ny, nx, nz = lax.axis_size("y"), lax.axis_size("x"), lax.axis_size("z")
    rows = 2 * ny * nx
    vertices = float(own * rows * nz)
    gains = weights.reshape(1, own)
    any_spec = pl.BlockSpec(memory_space=pl.ANY)
    flops = 2 * slots * k * tile * tile
    held = pltpu.VMEM((slots, tile, tile), BF16)
    sems = pltpu.SemaphoreType.DMA((slots,))
    panel_in = [SMEM] * 3 + [VMEM, any_spec]

    scaled, copies = call(
        prepare_kernel, [((k, own), BF16), ((rows, k, own), BF16)], [VMEM] * 2
    )(x_start, gains)
    gram = None
    for sweep in range(2):
        with jax.named_scope("gather_plane"):
            col_panel = exchange(copies, ROW)
        with jax.named_scope("gather_line"):
            row_panel = lax.all_gather(scaled, "z", axis=0)
        col_panel, row_panel = lax.optimization_barrier((col_panel, row_panel))
        with jax.named_scope("mirror"):
            keep, send = call(
                mirror_kernel,
                [((ny * nx, k, own), BF16)] * 2,
                panel_in,
                [held, pltpu.VMEM((rows, k, own), F32), sems],
                flops,
                blocks.size * 2,
            )(block_rows, block_cols, live_blocks, row_panel, blocks)
        with jax.named_scope("core_swap"):
            got = swap(send, "core", 1, 2)
        col_panel, send = lax.optimization_barrier((col_panel, send))
        with jax.named_scope("direct"):
            (direct,) = call(
                direct_kernel,
                [((nz, k, own), BF16)],
                panel_in,
                [held, pltpu.VMEM((nz, k, own), F32), sems],
                flops,
                blocks.size * 2,
            )(block_rows, block_cols, live_blocks, col_panel, blocks)
        with jax.named_scope("reduce_line"):
            arrived = exchange(direct, "z")
        with jax.named_scope("reduce_x"):
            pieces = call(merge_x_kernel, [((ny, k, own), BF16)] * nx, [VMEM] * 2)(keep, got)
            moved = [pieces[0]] + [swap(pieces[s], "x", s, nx) for s in range(1, nx)]
        with jax.named_scope("reduce_y"):
            pieces = call(merge_y_kernel, [((k, own), BF16)] * ny, [VMEM] * nx)(*moved)
            moved = [pieces[0]] + [swap(pieces[s], "y", s, ny) for s in range(1, ny)]
        if sweep == 0:
            with jax.named_scope("between"):
                scaled, copies, gram = call(
                    between_kernel,
                    [((k, own), BF16), ((rows, k, own), BF16), ((k, k), F32)],
                    [VMEM] * 6,
                )(arrived, gains, *moved)
        else:
            with jax.named_scope("last"):
                fresh, keep, send = call(
                    functools.partial(last_kernel, 1.0 / vertices),
                    [((k, own), BF16)] + [((k // 4, 2 * k), F32)] * 2,
                    [VMEM] * 7,
                )(arrived, gains, *moved, gram)
    with jax.named_scope("gram_core"):
        part = keep + swap(send, "core", 1, 2)
    with jax.named_scope("gram_plane"):
        copies = jnp.broadcast_to(part[None], (ny * nx,) + part.shape)
        part = jnp.sum(exchange(copies, ("y", "x")), axis=0)
    with jax.named_scope("gram_line"):
        copies = jnp.broadcast_to(part[None], (nz,) + part.shape)
        part = jnp.sum(exchange(copies, "z"), axis=0)
    with jax.named_scope("gram_pair"):
        parts = lax.all_gather(part, "core", axis=0)
    with jax.named_scope("whiten"):
        (out,) = call(
            whiten_kernel,
            [((k, own), BF16)],
            [VMEM] * 2,
            [pltpu.VMEM((k, 2 * k), F32)],
        )(parts, fresh)
    return out


def solution(mesh):
    fine = Mesh(mesh.devices.reshape(4, 4, 2, 16), ("y", "x", "core", "z"))
    cells = ("y", "x", "core", "z")
    return jax.shard_map(
        body,
        mesh=fine,
        in_specs=(P(None, cells), P(cells), P(cells, None, None), P(cells), P(cells), P(cells)),
        out_specs=P(None, cells),
        check_vma=False,
    )
```

```python
import functools

import jax
import jax.numpy as jnp
from jax import lax
from jax.experimental import pallas as pl
from jax.experimental.pallas import tpu as pltpu
from jax.sharding import Mesh, PartitionSpec as P

F32 = jnp.float32
BF16 = jnp.bfloat16
ROW = ("y", "x", "core")
LINE = ("far", "near")
RIDGE = 1e-06
STEP = 8
VMEM = pl.BlockSpec(memory_space=pltpu.VMEM)
SMEM = pl.BlockSpec(memory_space=pltpu.SMEM)
PARAMS = pltpu.CompilerParams(vmem_limit_bytes=48 * 1024 * 1024)
NT = (((1,), (1,)), ((), ()))
NN = (((1,), (0,)), ((), ()))


def call(kernel, outs, ins, scratch=(), flops=0, moved=0):
    return pl.pallas_call(
        kernel,
        out_shape=[jax.ShapeDtypeStruct(s, d) for s, d in outs],
        in_specs=ins,
        out_specs=[VMEM] * len(outs),
        scratch_shapes=list(scratch),
        compiler_params=PARAMS,
        cost_estimate=pl.CostEstimate(flops=flops, bytes_accessed=moved, transcendentals=0),
    )


def products_kernel(
    places, row_panel, col_panel, tiles, direct, keep, send, blocks, row_sum, col_sum, tile_sems
):
    slots = tiles.shape[0]
    copies = [pltpu.make_async_copy(tiles.at[s], blocks.at[s], tile_sems.at[s]) for s in range(slots)]
    for copy in copies:
        copy.start()
    row_sum[...] = jnp.zeros_like(row_sum)
    col_sum[...] = jnp.zeros_like(col_sum)
    half = row_panel.shape[2]
    for s, copy in enumerate(copies):
        copy.wait()

        @pl.when(s < places[2 * slots])
        def _():
            r, c = places[s], places[slots + s]
            low, high = 2 * r, 2 * r + 1
            left, right = 2 * c, 2 * c + 1
            part = lax.dot_general(
                row_panel[low], blocks[s, :half, :], NN, preferred_element_type=F32
            ) + lax.dot_general(row_panel[high], blocks[s, half:, :], NN, preferred_element_type=F32)
            col_sum[left] += part[:, :half]
            col_sum[right] += part[:, half:]
            part = lax.dot_general(
                col_panel[left], blocks[s, :, :half], NT, preferred_element_type=F32
            ) + lax.dot_general(col_panel[right], blocks[s, :, half:], NT, preferred_element_type=F32)
            row_sum[low] += part[:, :half]
            row_sum[high] += part[:, half:]

    direct[...] = row_sum[...].astype(BF16)
    me = lax.axis_index("core")
    for chip in range(keep.shape[0]):
        keep[chip] = col_sum[2 * chip + me].astype(BF16)
        send[chip] = col_sum[2 * chip + 1 - me].astype(BF16)


def merge_x_kernel(keep, got, *pieces):
    me = lax.axis_index("x")
    n = len(pieces)
    for k, piece in enumerate(pieces):
        to = lax.rem(me + k, n)
        for y in range(piece.shape[0]):
            piece[y] = (keep[y * n + to].astype(F32) + got[y * n + to].astype(F32)).astype(BF16)


def merge_y_kernel(own, *refs):
    n = own.shape[0]
    got, pieces = refs[: n - 1], refs[n - 1 :]
    me = lax.axis_index("y")
    for k, piece in enumerate(pieces):
        to = lax.rem(me + k, n)
        sums = own[to].astype(F32)
        for g in got:
            sums += g[to].astype(F32)
        piece[...] = sums.astype(BF16)


def spread(value, scaled, copies):
    scaled[...] = value
    for k in range(copies.shape[0]):
        copies[k] = value


def add_up(arrived, own, others, weights):
    sums = own[...].astype(F32)
    for other in others:
        sums += other[...].astype(F32)
    for k in range(arrived.shape[0]):
        sums += arrived[k].astype(F32)
    return sums * weights[...]


def between_kernel(arrived, own, s1, s2, s3, weights, scaled, copies, gram):
    fresh = add_up(arrived, own, (s1, s2, s3), weights)
    spread((fresh * weights[...]).astype(BF16), scaled, copies)
    rounded = fresh.astype(BF16)
    gram[...] = lax.dot_general(rounded, rounded, NT, preferred_element_type=F32)


def masks(h):
    i = lax.broadcasted_iota(jnp.int32, (h, h), 0)
    j = lax.broadcasted_iota(jnp.int32, (h, h), 1)
    return (i >= j).astype(F32), (i == j).astype(F32)


def pack(gram):
    h = gram.shape[0] // 2
    lower, eye = masks(h)
    mixed = gram[:h, :h] * lower + gram[h:, h:] * (1.0 - lower)
    diagonal = jnp.sum(gram[h:, h:] * eye, axis=0, keepdims=True)
    lines = []
    for block in (mixed, gram[h:, :h]):
        wide = jnp.concatenate([block[8 * i : 8 * i + 8] for i in range(h // 8)], axis=1)
        lines += [wide[i : i + 1] for i in range(8)]
    lines.append(jnp.concatenate([diagonal] * (128 // h), axis=1))
    lines.append(jnp.zeros_like(lines[-1]))
    return jnp.concatenate(lines, axis=1)


def unpack(row, n):
    h = n // 2
    lower, eye = masks(h)
    blocks = []
    for b in range(2):
        at = [row[:, 128 * (8 * b + i) : 128 * (8 * b + i + 1)] for i in range(8)]
        wide = jnp.concatenate(at, axis=0)
        blocks.append(jnp.concatenate([wide[:, h * i : h * i + h] for i in range(h // 8)], axis=0))
    mixed, corner = blocks
    diagonal = row[:, 2048 : 2048 + h] * eye
    upper = mixed * (1.0 - lower)
    strict = mixed * (lower - eye)
    first = strict + strict.T + mixed * eye
    second = upper + upper.T + diagonal
    return jnp.concatenate(
        [jnp.concatenate([first, corner.T], axis=1), jnp.concatenate([corner, second], axis=1)],
        axis=0,
    )


def last_kernel(scale, arrived, own, s1, s2, s3, weights, first, fresh, keep, send):
    rounded = add_up(arrived, own, (s1, s2, s3), weights).astype(BF16)
    fresh[...] = rounded
    gram = lax.dot_general(rounded, rounded, NT, preferred_element_type=F32)
    packed = pack((gram + RIDGE * first[...]) * scale)
    h = packed.shape[1] // 2
    second = lax.axis_index("core") == 1
    keep[...] = jnp.where(second, packed[:, h:], packed[:, :h])
    send[...] = jnp.where(second, packed[:, :h], packed[:, h:])


def whiten_kernel(parts, fresh, out, factor):
    packed = jnp.concatenate([parts[0], parts[1]], axis=1)
    n = fresh.shape[0]
    matrix = unpack(packed, n)
    eye = masks(n)[1]
    left = jnp.concatenate([matrix + RIDGE * RIDGE * eye, eye], axis=1)
    base = 0
    for j in range(0, n, STEP):
        if j - base == 8:
            left = left[8:]
            base = j
        i = j - base
        wide = (left.shape[0], 2 * n)
        cols = [jnp.broadcast_to(left[:, j + a : j + a + 1], wide) for a in range(STEP)]
        rows = [left[i + a : i + a + 1] for a in range(STEP)]
        block = [[cols[b][i + a : i + a + 1] for b in range(STEP)] for a in range(STEP)]
        for a in range(STEP):
            pivot = block[a][a]
            inverse = 1.0 / pivot
            for b in range(a + 1, STEP):
                ratio = block[a][b] * inverse
                for c in range(b, STEP):
                    block[b][c] = block[b][c] - ratio * block[a][c]
                rows[b] = rows[b] - ratio * rows[a]
                cols[b] = cols[b] - ratio * cols[a]
            factor[j + a : j + a + 1] = rows[a] * (1.0 / jnp.sqrt(pivot))
            rows[a] = rows[a] * inverse
        for a in range(STEP):
            left = left - cols[a] * rows[a]
    inverse = factor[:, n:]
    out[...] = lax.dot_general(
        inverse,
        fresh[...].astype(F32),
        NN,
        precision=lax.Precision.HIGHEST,
        preferred_element_type=F32,
    ).astype(BF16)


def shift(value, axis, step, size):
    return lax.ppermute(value, axis, [(i, (i + step) % size) for i in range(size)])


def exchange(value, axes):
    return lax.all_to_all(value, axes, split_axis=0, concat_axis=0, tiled=True)


def body(x_start, weights, blocks, block_rows, block_cols, live_blocks):
    k, own = x_start.shape
    slots, tile, _ = blocks.shape
    ny, nx, nz = lax.axis_size("y"), lax.axis_size("x"), lax.axis_size("far") * lax.axis_size("near")
    rows = 2 * ny * nx
    vertices = float(own * rows * nz)
    gains = weights.reshape(1, own)
    any_spec = pl.BlockSpec(memory_space=pl.ANY)
    any_in = pl.BlockSpec(memory_space=pltpu.HBM)
    places = jnp.concatenate([block_rows, block_cols, live_blocks])
    scaled = (x_start.astype(F32) * gains).astype(BF16)
    copies = jnp.broadcast_to(scaled[None], (rows, k, own))
    gram = None
    for sweep in range(2):
        with jax.named_scope("gather_plane"):
            col_panel = exchange(copies, ROW)
        with jax.named_scope("gather_line"):
            row_panel = lax.all_gather(scaled, LINE, axis=0)
        col_panel, row_panel = lax.optimization_barrier((col_panel, row_panel))
        with jax.named_scope("products"):
            direct, keep, send = call(
                products_kernel,
                [((nz, k, own), BF16)] + [((ny * nx, k, own), BF16)] * 2,
                [SMEM] + [VMEM] * 2 + [any_in],
                [pltpu.VMEM((slots, tile, tile), BF16)]
                + [pltpu.VMEM((nz, k, own), F32), pltpu.VMEM((rows, k, own), F32)]
                + [pltpu.SemaphoreType.DMA((slots,))],
                4 * slots * k * tile * tile,
                blocks.size * 2,
            )(places, row_panel, col_panel, blocks)
        with jax.named_scope("reduce_core"):
            got = shift(send, "core", 1, 2)
        direct, got = lax.optimization_barrier((direct, got))
        with jax.named_scope("reduce_line"):
            arrived = exchange(direct, LINE)
        with jax.named_scope("reduce_x"):
            pieces = call(merge_x_kernel, [((ny, k, own), BF16)] * nx, [VMEM] * 2)(keep, got)
            moved = [pieces[0]] + [shift(pieces[s], "x", s, nx) for s in range(1, nx)]
        with jax.named_scope("reduce_y"):
            pieces = call(merge_y_kernel, [((k, own), BF16)] * ny, [VMEM] * nx)(*moved)
            moved = [pieces[0]] + [shift(pieces[s], "y", s, ny) for s in range(1, ny)]
        if sweep == 0:
            with jax.named_scope("between"):
                scaled, copies, gram = call(
                    between_kernel,
                    [((k, own), BF16), ((rows, k, own), BF16), ((k, k), F32)],
                    [VMEM] * 6,
                )(arrived, *moved, gains)
        else:
            with jax.named_scope("last"):
                fresh, keep, send = call(
                    functools.partial(last_kernel, 1.0 / vertices),
                    [((k, own), BF16)] + [((1, 9 * 128), F32)] * 2,
                    [VMEM] * 7,
                )(arrived, *moved, gains, gram)
    with jax.named_scope("gram_core"):
        part = keep + shift(send, "core", 1, 2)
    with jax.named_scope("gram_plane"):
        copies = jnp.broadcast_to(part[None], (ny * nx,) + part.shape)
        part = jnp.sum(exchange(copies, ("y", "x")), axis=0)
    with jax.named_scope("gram_line"):
        copies = jnp.broadcast_to(part[None], (nz,) + part.shape)
        part = jnp.sum(exchange(copies, LINE), axis=0)
    with jax.named_scope("gram_pair"):
        parts = lax.all_gather(part, "core", axis=0)
    with jax.named_scope("whiten"):
        (out,) = call(
            whiten_kernel,
            [((k, own), BF16)],
            [VMEM] * 2,
            [pltpu.VMEM((k, 2 * k), F32)],
        )(parts, fresh)
    return out


def solution(mesh):
    cells = ROW + LINE
    fine = Mesh(mesh.devices.reshape(4, 4, 2, 8, 2), cells)
    return jax.shard_map(
        body,
        mesh=fine,
        in_specs=(P(None, cells), P(cells), P(cells, None, None), P(cells), P(cells), P(cells)),
        out_specs=P(None, cells),
        check_vma=False,
    )
```

```python
import functools

import jax
import jax.numpy as jnp
from jax import lax
from jax.experimental import pallas as pl
from jax.experimental.pallas import tpu as pltpu
from jax.sharding import Mesh, PartitionSpec as P

F32 = jnp.float32
BF16 = jnp.bfloat16
ROW = ("y", "x", "core")
LINE = ("far", "near")
RIDGE = 1e-06
STEP = 8
VMEM = pl.BlockSpec(memory_space=pltpu.VMEM)
SMEM = pl.BlockSpec(memory_space=pltpu.SMEM)
PARAMS = pltpu.CompilerParams(vmem_limit_bytes=48 * 1024 * 1024)
NT = (((1,), (1,)), ((), ()))
NN = (((1,), (0,)), ((), ()))


def call(kernel, outs, ins, scratch=(), flops=0, moved=0):
    return pl.pallas_call(
        kernel,
        out_shape=[jax.ShapeDtypeStruct(s, d) for s, d in outs],
        in_specs=ins,
        out_specs=[VMEM] * len(outs),
        scratch_shapes=list(scratch),
        compiler_params=PARAMS,
        cost_estimate=pl.CostEstimate(flops=flops, bytes_accessed=moved, transcendentals=0),
    )


def products_kernel(
    places, row_panel, col_panel, tiles, direct, keep, send, blocks, row_sum, col_sum, tile_sems
):
    slots = tiles.shape[0]
    copies = [pltpu.make_async_copy(tiles.at[s], blocks.at[s], tile_sems.at[s]) for s in range(slots)]
    for s, copy in enumerate(copies):
        pl.when(s < places[2 * slots])(copy.start)
    row_sum[...] = jnp.zeros_like(row_sum)
    col_sum[...] = jnp.zeros_like(col_sum)
    half = row_panel.shape[2]
    for s, copy in enumerate(copies):

        @pl.when(s < places[2 * slots])
        def _():
            copy.wait()
            r, c = places[s], places[slots + s]
            low, high = 2 * r, 2 * r + 1
            left, right = 2 * c, 2 * c + 1
            part = lax.dot_general(
                row_panel[low], blocks[s, :half, :], NN, preferred_element_type=F32
            ) + lax.dot_general(row_panel[high], blocks[s, half:, :], NN, preferred_element_type=F32)
            col_sum[left] += part[:, :half]
            col_sum[right] += part[:, half:]
            part = lax.dot_general(
                col_panel[left], blocks[s, :, :half], NT, preferred_element_type=F32
            ) + lax.dot_general(col_panel[right], blocks[s, :, half:], NT, preferred_element_type=F32)
            row_sum[low] += part[:, :half]
            row_sum[high] += part[:, half:]

    direct[...] = row_sum[...].astype(BF16)
    me = lax.axis_index("core")
    for chip in range(keep.shape[0]):
        keep[chip] = col_sum[2 * chip + me].astype(BF16)
        send[chip] = col_sum[2 * chip + 1 - me].astype(BF16)


def merge_x_kernel(keep, got, *pieces):
    me = lax.axis_index("x")
    n = len(pieces)
    for k, piece in enumerate(pieces):
        to = lax.rem(me + k, n)
        for y in range(piece.shape[0]):
            piece[y] = (keep[y * n + to].astype(F32) + got[y * n + to].astype(F32)).astype(BF16)


def merge_y_kernel(own, *refs):
    n = own.shape[0]
    got, pieces = refs[: n - 1], refs[n - 1 :]
    me = lax.axis_index("y")
    for k, piece in enumerate(pieces):
        to = lax.rem(me + k, n)
        sums = own[to].astype(F32)
        for g in got:
            sums += g[to].astype(F32)
        piece[...] = sums.astype(BF16)


def spread(value, scaled, copies):
    scaled[...] = value
    for k in range(copies.shape[0]):
        copies[k] = value


def add_up(arrived, own, others, weights):
    sums = own[...].astype(F32)
    for other in others:
        sums += other[...].astype(F32)
    for k in range(arrived.shape[0]):
        sums += arrived[k].astype(F32)
    return sums * weights[...]


def between_kernel(arrived, own, s1, s2, s3, weights, scaled, copies, gram):
    fresh = add_up(arrived, own, (s1, s2, s3), weights)
    spread((fresh * weights[...]).astype(BF16), scaled, copies)
    rounded = fresh.astype(BF16)
    gram[...] = lax.dot_general(rounded, rounded, NT, preferred_element_type=F32)


def masks(h):
    i = lax.broadcasted_iota(jnp.int32, (h, h), 0)
    j = lax.broadcasted_iota(jnp.int32, (h, h), 1)
    return (i >= j).astype(F32), (i == j).astype(F32)


def pack(gram):
    h = gram.shape[0] // 2
    lower, eye = masks(h)
    mixed = gram[:h, :h] * lower + gram[h:, h:] * (1.0 - lower)
    diagonal = jnp.sum(gram[h:, h:] * eye, axis=0, keepdims=True)
    lines = []
    for block in (mixed, gram[h:, :h]):
        wide = jnp.concatenate([block[8 * i : 8 * i + 8] for i in range(h // 8)], axis=1)
        lines += [wide[i : i + 1] for i in range(8)]
    lines.append(jnp.concatenate([diagonal] * (128 // h), axis=1))
    lines.append(jnp.zeros_like(lines[-1]))
    return jnp.concatenate(lines, axis=1)


def unpack(row, n):
    h = n // 2
    lower, eye = masks(h)
    blocks = []
    for b in range(2):
        at = [row[:, 128 * (8 * b + i) : 128 * (8 * b + i + 1)] for i in range(8)]
        wide = jnp.concatenate(at, axis=0)
        blocks.append(jnp.concatenate([wide[:, h * i : h * i + h] for i in range(h // 8)], axis=0))
    mixed, corner = blocks
    diagonal = row[:, 2048 : 2048 + h] * eye
    upper = mixed * (1.0 - lower)
    strict = mixed * (lower - eye)
    first = strict + strict.T + mixed * eye
    second = upper + upper.T + diagonal
    return jnp.concatenate(
        [jnp.concatenate([first, corner.T], axis=1), jnp.concatenate([corner, second], axis=1)],
        axis=0,
    )


def last_kernel(scale, arrived, own, s1, s2, s3, weights, first, fresh, copies):
    rounded = add_up(arrived, own, (s1, s2, s3), weights).astype(BF16)
    fresh[...] = rounded
    gram = lax.dot_general(rounded, rounded, NT, preferred_element_type=F32)
    packed = pack((gram + RIDGE * first[...]) * scale)
    h = packed.shape[1] // 2
    for k in range(copies.shape[0]):
        copies[k] = packed[:, h:] if k % 2 else packed[:, :h]


def whiten_kernel(parts, fresh, out, factor):
    packed = jnp.concatenate([parts[0], parts[1]], axis=1)
    n = fresh.shape[0]
    matrix = unpack(packed, n)
    eye = masks(n)[1]
    left = jnp.concatenate([matrix + RIDGE * RIDGE * eye, eye], axis=1)
    base = 0
    for j in range(0, n, STEP):
        if j - base == 8:
            left = left[8:]
            base = j
        i = j - base
        wide = (left.shape[0], 2 * n)
        cols = [jnp.broadcast_to(left[:, j + a : j + a + 1], wide) for a in range(STEP)]
        rows = [left[i + a : i + a + 1] for a in range(STEP)]
        block = [[cols[b][i + a : i + a + 1] for b in range(STEP)] for a in range(STEP)]
        for a in range(STEP):
            pivot = block[a][a]
            inverse = 1.0 / pivot
            for b in range(a + 1, STEP):
                ratio = block[a][b] * inverse
                for c in range(b, STEP):
                    block[b][c] = block[b][c] - ratio * block[a][c]
                rows[b] = rows[b] - ratio * rows[a]
                cols[b] = cols[b] - ratio * cols[a]
            factor[j + a : j + a + 1] = rows[a] * (1.0 / jnp.sqrt(pivot))
            rows[a] = rows[a] * inverse
        for a in range(STEP):
            left = left - cols[a] * rows[a]
    inverse = factor[:, n:]
    out[...] = lax.dot_general(
        inverse,
        fresh[...].astype(F32),
        NN,
        precision=lax.Precision.HIGHEST,
        preferred_element_type=F32,
    ).astype(BF16)


def shift(value, axis, step, size):
    return lax.ppermute(value, axis, [(i, (i + step) % size) for i in range(size)])


def exchange(value, axes):
    return lax.all_to_all(value, axes, split_axis=0, concat_axis=0, tiled=True)


def body(x_start, weights, blocks, block_rows, block_cols, live_blocks):
    k, own = x_start.shape
    slots, tile, _ = blocks.shape
    ny, nx, nz = lax.axis_size("y"), lax.axis_size("x"), lax.axis_size("far") * lax.axis_size("near")
    rows = 2 * ny * nx
    vertices = float(own * rows * nz)
    gains = weights.reshape(1, own)
    any_spec = pl.BlockSpec(memory_space=pl.ANY)
    any_in = pl.BlockSpec(memory_space=pltpu.HBM)
    places = jnp.concatenate([block_rows, block_cols, live_blocks])
    scaled = (x_start.astype(F32) * gains).astype(BF16)
    copies = jnp.broadcast_to(scaled[None], (rows, k, own))
    gram = None
    for sweep in range(2):
        with jax.named_scope("gather_plane"):
            col_panel = exchange(copies, ROW)
        with jax.named_scope("gather_line"):
            row_panel = lax.all_gather(scaled, LINE, axis=0)
        col_panel, row_panel = lax.optimization_barrier((col_panel, row_panel))
        with jax.named_scope("products"):
            direct, keep, send = call(
                products_kernel,
                [((nz, k, own), BF16)] + [((ny * nx, k, own), BF16)] * 2,
                [SMEM] + [VMEM] * 2 + [any_in],
                [pltpu.VMEM((slots, tile, tile), BF16)]
                + [pltpu.VMEM((nz, k, own), F32), pltpu.VMEM((rows, k, own), F32)]
                + [pltpu.SemaphoreType.DMA((slots,))],
                4 * slots * k * tile * tile,
                blocks.size * 2,
            )(places, row_panel, col_panel, blocks)
        with jax.named_scope("reduce_core"):
            got = shift(send, "core", 1, 2)
        direct, got = lax.optimization_barrier((direct, got))
        with jax.named_scope("reduce_line"):
            arrived = exchange(direct, LINE)
        with jax.named_scope("reduce_x"):
            pieces = call(merge_x_kernel, [((ny, k, own), BF16)] * nx, [VMEM] * 2)(keep, got)
            moved = [pieces[0]] + [shift(pieces[s], "x", s, nx) for s in range(1, nx)]
        with jax.named_scope("reduce_y"):
            pieces = call(merge_y_kernel, [((k, own), BF16)] * ny, [VMEM] * nx)(*moved)
            moved = [pieces[0]] + [shift(pieces[s], "y", s, ny) for s in range(1, ny)]
        if sweep == 0:
            with jax.named_scope("between"):
                scaled, copies, gram = call(
                    between_kernel,
                    [((k, own), BF16), ((rows, k, own), BF16), ((k, k), F32)],
                    [VMEM] * 6,
                )(arrived, *moved, gains)
        else:
            with jax.named_scope("last"):
                fresh, copies = call(
                    functools.partial(last_kernel, 1.0 / vertices),
                    [((k, own), BF16), ((rows, 1, 9 * 128), F32)],
                    [VMEM] * 7,
                )(arrived, *moved, gains, gram)
    with jax.named_scope("gram_plane"):
        part = jnp.sum(exchange(copies, ROW), axis=0)
    with jax.named_scope("gram_line"):
        copies = jnp.broadcast_to(part[None], (nz,) + part.shape)
        part = jnp.sum(exchange(copies, LINE), axis=0)
    with jax.named_scope("gram_pair"):
        parts = lax.all_gather(part, "core", axis=0)
    with jax.named_scope("whiten"):
        (out,) = call(
            whiten_kernel,
            [((k, own), BF16)],
            [VMEM] * 2,
            [pltpu.VMEM((k, 2 * k), F32)],
        )(parts, fresh)
    return out


def solution(mesh):
    cells = ROW + LINE
    fine = Mesh(mesh.devices.reshape(4, 4, 2, 8, 2), cells)
    return jax.shard_map(
        body,
        mesh=fine,
        in_specs=(P(None, cells), P(cells), P(cells, None, None), P(cells), P(cells), P(cells)),
        out_specs=P(None, cells),
        check_vma=False,
    )
```

```python
import functools

import jax
import jax.numpy as jnp
from jax import lax
from jax.experimental import pallas as pl
from jax.experimental.pallas import tpu as pltpu
from jax.sharding import Mesh, PartitionSpec as P

F32 = jnp.float32
BF16 = jnp.bfloat16
ROW = ("y", "x", "core")
LINE = ("far", "mid", "near")
RIDGE = 1e-06
STEP = 8
LONG = 1 << 44
VMEM = pl.BlockSpec(memory_space=pltpu.VMEM)
SMEM = pl.BlockSpec(memory_space=pltpu.SMEM)
MIB = 1024 * 1024
NT = (((1,), (1,)), ((), ()))
NN = (((1,), (0,)), ((), ()))


def call(kernel, outs, ins, scratch=(), flops=0, moved=0, room=16):
    return pl.pallas_call(
        kernel,
        out_shape=[jax.ShapeDtypeStruct(s, d) for s, d in outs],
        in_specs=ins,
        out_specs=[VMEM] * len(outs),
        scratch_shapes=list(scratch),
        compiler_params=pltpu.CompilerParams(vmem_limit_bytes=room * MIB),
        cost_estimate=pl.CostEstimate(flops=flops, bytes_accessed=moved, transcendentals=0),
    )


def products_kernel(
    places, row_panel, col_panel, tiles, plane_keep, plane_send, keep, send,
    blocks, row_sum, col_sum, tile_sems,
):
    slots = tiles.shape[0]
    copies = [pltpu.make_async_copy(tiles.at[s], blocks.at[s], tile_sems.at[s]) for s in range(slots)]
    for s, copy in enumerate(copies):
        pl.when(s < places[2 * slots])(copy.start)
    row_sum[...] = jnp.zeros_like(row_sum)
    col_sum[...] = jnp.zeros_like(col_sum)
    half = row_panel.shape[2]
    for s, copy in enumerate(copies):

        @pl.when(s < places[2 * slots])
        def _():
            copy.wait()
            r, c = places[s], places[slots + s]
            low, high = 2 * r, 2 * r + 1
            left, right = 2 * c, 2 * c + 1
            part = lax.dot_general(
                row_panel[low], blocks[s, :half, :], NN, preferred_element_type=F32
            ) + lax.dot_general(row_panel[high], blocks[s, half:, :], NN, preferred_element_type=F32)
            col_sum[left] += part[:, :half]
            col_sum[right] += part[:, half:]
            part = lax.dot_general(
                col_panel[left], blocks[s, :, :half], NT, preferred_element_type=F32
            ) + lax.dot_general(col_panel[right], blocks[s, :, half:], NT, preferred_element_type=F32)
            row_sum[low] += part[:, :half]
            row_sum[high] += part[:, half:]

    me = lax.axis_index("core")
    for chip in range(plane_keep.shape[0]):
        plane_keep[chip] = col_sum[2 * chip + me].astype(BF16)
        plane_send[chip] = col_sum[2 * chip + 1 - me].astype(BF16)
    me = lax.axis_index("near")
    for pair in range(keep.shape[0]):
        keep[pair] = row_sum[2 * pair + me].astype(BF16)
        send[pair] = row_sum[2 * pair + 1 - me].astype(BF16)


def sum_kernel(keep, got, out):
    out[...] = (keep[...].astype(F32) + got[...].astype(F32)).astype(BF16)


def total_kernel(pieces, out):
    sums = pieces[0].astype(F32)
    for k in range(1, pieces.shape[0]):
        sums += pieces[k].astype(F32)
    out[...] = sums


def halve_kernel(keep, got, stay, go):
    me = lax.axis_index("mid")
    for pair in range(stay.shape[0]):
        for out, at in ((stay, 2 * pair + me), (go, 2 * pair + 1 - me)):
            out[pair] = (keep[at].astype(F32) + got[at].astype(F32)).astype(BF16)


def spread(value, scaled, copies):
    scaled[...] = value
    for k in range(copies.shape[0]):
        copies[k] = value


def add_up(from_line, from_plane, weights):
    sums = from_plane[...]
    for k in range(from_line.shape[0]):
        sums += from_line[k].astype(F32)
    return sums * weights[...]


def between_kernel(from_line, from_plane, weights, scaled, copies, gram):
    fresh = add_up(from_line, from_plane, weights)
    spread((fresh * weights[...]).astype(BF16), scaled, copies)
    rounded = fresh.astype(BF16)
    gram[...] = lax.dot_general(rounded, rounded, NT, preferred_element_type=F32)


def masks(h):
    i = lax.broadcasted_iota(jnp.int32, (h, h), 0)
    j = lax.broadcasted_iota(jnp.int32, (h, h), 1)
    return (i >= j).astype(F32), (i == j).astype(F32)


def pack(gram):
    h = gram.shape[0] // 2
    lower, eye = masks(h)
    mixed = gram[:h, :h] * lower + gram[h:, h:] * (1.0 - lower)
    diagonal = jnp.sum(gram[h:, h:] * eye, axis=0, keepdims=True)
    lines = []
    for block in (mixed, gram[h:, :h]):
        wide = jnp.concatenate([block[8 * i : 8 * i + 8] for i in range(h // 8)], axis=1)
        lines += [wide[i : i + 1] for i in range(8)]
    lines.append(jnp.concatenate([diagonal] * (128 // h), axis=1))
    lines.append(jnp.zeros_like(lines[-1]))
    return jnp.concatenate(lines, axis=1)


def unpack(row, n):
    h = n // 2
    lower, eye = masks(h)
    blocks = []
    for b in range(2):
        at = [row[:, 128 * (8 * b + i) : 128 * (8 * b + i + 1)] for i in range(8)]
        wide = jnp.concatenate(at, axis=0)
        blocks.append(jnp.concatenate([wide[:, h * i : h * i + h] for i in range(h // 8)], axis=0))
    mixed, corner = blocks
    diagonal = row[:, 2048 : 2048 + h] * eye
    upper = mixed * (1.0 - lower)
    strict = mixed * (lower - eye)
    first = strict + strict.T + mixed * eye
    second = upper + upper.T + diagonal
    return jnp.concatenate(
        [jnp.concatenate([first, corner.T], axis=1), jnp.concatenate([corner, second], axis=1)],
        axis=0,
    )


def last_kernel(scale, from_line, from_plane, weights, first, fresh, copies):
    rounded = add_up(from_line, from_plane, weights).astype(BF16)
    fresh[...] = rounded
    gram = lax.dot_general(rounded, rounded, NT, preferred_element_type=F32)
    packed = pack((gram + RIDGE * first[...]) * scale)
    h = packed.shape[1] // 2
    for k in range(copies.shape[0]):
        copies[k] = packed[:, h:] if k % 2 else packed[:, :h]


def whiten_kernel(parts, fresh, out, factor):
    packed = jnp.concatenate([parts[0], parts[1]], axis=1)
    n = fresh.shape[0]
    matrix = unpack(packed, n)
    eye = masks(n)[1]
    left = jnp.concatenate([matrix + RIDGE * RIDGE * eye, eye], axis=1)
    base = 0
    for j in range(0, n, STEP):
        if j - base == 8:
            left = left[8:]
            base = j
        i = j - base
        wide = (left.shape[0], 2 * n)
        cols = [jnp.broadcast_to(left[:, j + a : j + a + 1], wide) for a in range(STEP)]
        rows = [left[i + a : i + a + 1] for a in range(STEP)]
        block = [[cols[b][i + a : i + a + 1] for b in range(STEP)] for a in range(STEP)]
        for a in range(STEP):
            pivot = block[a][a]
            inverse = 1.0 / pivot
            for b in range(a + 1, STEP):
                ratio = block[a][b] * inverse
                for c in range(b, STEP):
                    block[b][c] = block[b][c] - ratio * block[a][c]
                rows[b] = rows[b] - ratio * rows[a]
                cols[b] = cols[b] - ratio * cols[a]
            factor[j + a : j + a + 1] = rows[a] * (1.0 / jnp.sqrt(pivot))
            rows[a] = rows[a] * inverse
        for a in range(STEP):
            left = left - cols[a] * rows[a]
    inverse = factor[:, n:]
    out[...] = lax.dot_general(
        inverse,
        fresh[...].astype(F32),
        NN,
        precision=lax.Precision.HIGHEST,
        preferred_element_type=F32,
    ).astype(BF16)


def shift(value, axis, step, size):
    return lax.ppermute(value, axis, [(i, (i + step) % size) for i in range(size)])


def exchange(value, axes):
    return lax.all_to_all(value, axes, split_axis=0, concat_axis=0, tiled=True)


def body(x_start, weights, blocks, block_rows, block_cols, live_blocks):
    k, own = x_start.shape
    slots, tile, _ = blocks.shape
    ny, nx, nz = lax.axis_size("y"), lax.axis_size("x"), lax.axis_size(LINE)
    rows = 2 * ny * nx
    vertices = float(own * rows * nz)
    gains = weights.reshape(1, own)
    any_spec = pl.BlockSpec(memory_space=pl.ANY)
    any_in = pl.BlockSpec(memory_space=pltpu.HBM)
    places = jnp.concatenate([block_rows, block_cols, live_blocks])
    scaled = (x_start.astype(F32) * gains).astype(BF16)
    copies = jnp.broadcast_to(scaled[None], (rows, k, own))
    gram = None
    for sweep in range(2):
        with jax.named_scope("gather_plane"):
            col_panel = exchange(copies, ROW)
        with jax.named_scope("gather_line"):
            row_panel = lax.all_gather(scaled, LINE, axis=0)
        col_panel, row_panel = lax.optimization_barrier((col_panel, row_panel))
        with jax.named_scope("products"):
            plane_keep, plane_send, keep, send = call(
                products_kernel,
                [((ny * nx, k, own), BF16)] * 2 + [((nz // 2, k, own), BF16)] * 2,
                [SMEM] + [VMEM] * 2 + [any_in],
                [pltpu.VMEM((slots, tile, tile), BF16)]
                + [pltpu.VMEM((nz, k, own), F32), pltpu.VMEM((rows, k, own), F32)]
                + [pltpu.SemaphoreType.DMA((slots,))],
                4 * slots * k * tile * tile,
                blocks.size * 2,
                48,
            )(places, row_panel, col_panel, blocks)
        with jax.named_scope("reduce_near"):
            got = shift(send, "near", 1, 2)
        with jax.named_scope("reduce_plane"):
            plane_got = shift(plane_send, "core", 1, 2)
            (plane,) = call(sum_kernel, [((ny * nx, k, own), BF16)], [VMEM] * 2)(
                plane_keep, plane_got
            )
            (from_plane,) = call(total_kernel, [((k, own), F32)], [VMEM])(
                exchange(plane, ("y", "x"))
            )
        with jax.named_scope("reduce_mid"):
            keep, send = call(
                halve_kernel, [((nz // 4, k, own), BF16)] * 2, [VMEM] * 2, flops=LONG
            )(keep, got)
            got = shift(send, "mid", 1, 2)
        with jax.named_scope("reduce_far"):
            got, from_plane = lax.optimization_barrier((got, from_plane))
            line = (keep.astype(F32) + got.astype(F32)).astype(BF16)
            from_line = exchange(line, "far")
        if sweep == 0:
            with jax.named_scope("between"):
                scaled, copies, gram = call(
                    between_kernel,
                    [((k, own), BF16), ((rows, k, own), BF16), ((k, k), F32)],
                    [VMEM] * 3,
                )(from_line, from_plane, gains)
        else:
            with jax.named_scope("last"):
                fresh, copies = call(
                    functools.partial(last_kernel, 1.0 / vertices),
                    [((k, own), BF16), ((rows, 1, 9 * 128), F32)],
                    [VMEM] * 4,
                )(from_line, from_plane, gains, gram)
    with jax.named_scope("gram_plane"):
        part = jnp.sum(exchange(copies, ROW), axis=0)
    with jax.named_scope("gram_line"):
        copies = jnp.broadcast_to(part[None], (nz,) + part.shape)
        part = jnp.sum(exchange(copies, LINE), axis=0)
    with jax.named_scope("gram_pair"):
        parts = lax.all_gather(part, "core", axis=0)
    with jax.named_scope("whiten"):
        (out,) = call(
            whiten_kernel,
            [((k, own), BF16)],
            [VMEM] * 2,
            [pltpu.VMEM((k, 2 * k), F32)],
        )(parts, fresh)
    return out


def solution(mesh):
    cells = ROW + LINE
    fine = Mesh(mesh.devices.reshape(4, 4, 2, 4, 2, 2), cells)
    return jax.shard_map(
        body,
        mesh=fine,
        in_specs=(P(None, cells), P(cells), P(cells, None, None), P(cells), P(cells), P(cells)),
        out_specs=P(None, cells),
        check_vma=False,
    )
```

```python
import functools

import jax
import jax.numpy as jnp
from jax import lax
from jax.experimental import pallas as pl
from jax.experimental.pallas import tpu as pltpu
from jax.sharding import Mesh, PartitionSpec as P

F32 = jnp.float32
BF16 = jnp.bfloat16
ROW = ("y", "x", "core")
LINE = ("far", "mid", "near")
RIDGE = 1e-06
STEP = 8
LONG = 1 << 44
VMEM = pl.BlockSpec(memory_space=pltpu.VMEM)
SMEM = pl.BlockSpec(memory_space=pltpu.SMEM)
MIB = 1024 * 1024
NT = (((1,), (1,)), ((), ()))
NN = (((1,), (0,)), ((), ()))


def call(kernel, outs, ins, scratch=(), flops=0, moved=0, room=16):
    return pl.pallas_call(
        kernel,
        out_shape=[jax.ShapeDtypeStruct(s, d) for s, d in outs],
        in_specs=ins,
        out_specs=[VMEM] * len(outs),
        scratch_shapes=list(scratch),
        compiler_params=pltpu.CompilerParams(vmem_limit_bytes=room * MIB),
        cost_estimate=pl.CostEstimate(flops=flops, bytes_accessed=moved, transcendentals=0),
    )


def products_kernel(
    places, row_panel, near_panel, other_panel, tiles, plane_keep, plane_send, keep, send,
    blocks, row_sum, col_sum, tile_sems,
):
    slots = tiles.shape[0]
    copies = [pltpu.make_async_copy(tiles.at[s], blocks.at[s], tile_sems.at[s]) for s in range(slots)]
    for s, copy in enumerate(copies):
        pl.when(s < places[2 * slots])(copy.start)
    row_sum[...] = jnp.zeros_like(row_sum)
    col_sum[...] = jnp.zeros_like(col_sum)
    half = row_panel.shape[2]
    first = lax.axis_index("core") == 0
    for s, copy in enumerate(copies):

        @pl.when(s < places[2 * slots])
        def _():
            copy.wait()
            r, c = places[s], places[slots + s]
            low, high = 2 * r, 2 * r + 1
            left, right = 2 * c, 2 * c + 1
            part = lax.dot_general(
                row_panel[low], blocks[s, :half, :], NN, preferred_element_type=F32
            ) + lax.dot_general(row_panel[high], blocks[s, half:, :], NN, preferred_element_type=F32)
            col_sum[left] += part[:, :half]
            col_sum[right] += part[:, half:]
            own, other = near_panel[c], other_panel[c]
            part = lax.dot_general(
                jnp.where(first, own, other), blocks[s, :, :half], NT, preferred_element_type=F32
            ) + lax.dot_general(
                jnp.where(first, other, own), blocks[s, :, half:], NT, preferred_element_type=F32
            )
            row_sum[low] += part[:, :half]
            row_sum[high] += part[:, half:]

    me = lax.axis_index("core")
    for chip in range(plane_keep.shape[0]):
        plane_keep[chip] = col_sum[2 * chip + me].astype(BF16)
        plane_send[chip] = col_sum[2 * chip + 1 - me].astype(BF16)
    me = lax.axis_index("near")
    for pair in range(keep.shape[0]):
        keep[pair] = row_sum[2 * pair + me].astype(BF16)
        send[pair] = row_sum[2 * pair + 1 - me].astype(BF16)


def sum_kernel(keep, got, out):
    out[...] = (keep[...].astype(F32) + got[...].astype(F32)).astype(BF16)


def total_kernel(pieces, out):
    sums = pieces[0].astype(F32)
    for k in range(1, pieces.shape[0]):
        sums += pieces[k].astype(F32)
    out[...] = sums


def halve_kernel(keep, got, stay, go):
    me = lax.axis_index("mid")
    for pair in range(stay.shape[0]):
        for out, at in ((stay, 2 * pair + me), (go, 2 * pair + 1 - me)):
            out[pair] = (keep[at].astype(F32) + got[at].astype(F32)).astype(BF16)


def spread(value, scaled, copies):
    scaled[...] = value
    for k in range(copies.shape[0]):
        copies[k] = value


def add_up(from_line, from_plane, weights):
    sums = from_plane[...]
    for k in range(from_line.shape[0]):
        sums += from_line[k].astype(F32)
    return sums * weights[...]


def between_kernel(from_line, from_plane, weights, scaled, copies, gram):
    fresh = add_up(from_line, from_plane, weights)
    spread((fresh * weights[...]).astype(BF16), scaled, copies)
    rounded = fresh.astype(BF16)
    gram[...] = lax.dot_general(rounded, rounded, NT, preferred_element_type=F32)


def masks(h):
    i = lax.broadcasted_iota(jnp.int32, (h, h), 0)
    j = lax.broadcasted_iota(jnp.int32, (h, h), 1)
    return (i >= j).astype(F32), (i == j).astype(F32)


def pack(gram):
    h = gram.shape[0] // 2
    lower, eye = masks(h)
    mixed = gram[:h, :h] * lower + gram[h:, h:] * (1.0 - lower)
    diagonal = jnp.sum(gram[h:, h:] * eye, axis=0, keepdims=True)
    lines = []
    for block in (mixed, gram[h:, :h]):
        wide = jnp.concatenate([block[8 * i : 8 * i + 8] for i in range(h // 8)], axis=1)
        lines += [wide[i : i + 1] for i in range(8)]
    lines.append(jnp.concatenate([diagonal] * (128 // h), axis=1))
    lines.append(jnp.zeros_like(lines[-1]))
    return jnp.concatenate(lines, axis=1)


def unpack(row, n):
    h = n // 2
    lower, eye = masks(h)
    blocks = []
    for b in range(2):
        at = [row[:, 128 * (8 * b + i) : 128 * (8 * b + i + 1)] for i in range(8)]
        wide = jnp.concatenate(at, axis=0)
        blocks.append(jnp.concatenate([wide[:, h * i : h * i + h] for i in range(h // 8)], axis=0))
    mixed, corner = blocks
    diagonal = row[:, 2048 : 2048 + h] * eye
    upper = mixed * (1.0 - lower)
    strict = mixed * (lower - eye)
    first = strict + strict.T + mixed * eye
    second = upper + upper.T + diagonal
    return jnp.concatenate(
        [jnp.concatenate([first, corner.T], axis=1), jnp.concatenate([corner, second], axis=1)],
        axis=0,
    )


def last_kernel(scale, from_line, from_plane, weights, first, fresh, copies):
    rounded = add_up(from_line, from_plane, weights).astype(BF16)
    fresh[...] = rounded
    gram = lax.dot_general(rounded, rounded, NT, preferred_element_type=F32)
    packed = pack((gram + RIDGE * first[...]) * scale)
    h = packed.shape[1] // 2
    for k in range(copies.shape[0]):
        copies[k] = packed[:, h:] if k % 2 else packed[:, :h]


def whiten_kernel(parts, fresh, out, factor):
    packed = jnp.concatenate([parts[0], parts[1]], axis=1)
    n = fresh.shape[0]
    matrix = unpack(packed, n)
    eye = masks(n)[1]
    left = jnp.concatenate([matrix + RIDGE * RIDGE * eye, eye], axis=1)
    base = 0
    for j in range(0, n, STEP):
        if j - base == 8:
            left = left[8:]
            base = j
        i = j - base
        wide = (left.shape[0], 2 * n)
        cols = [jnp.broadcast_to(left[:, j + a : j + a + 1], wide) for a in range(STEP)]
        rows = [left[i + a : i + a + 1] for a in range(STEP)]
        block = [[cols[b][i + a : i + a + 1] for b in range(STEP)] for a in range(STEP)]
        for a in range(STEP):
            pivot = block[a][a]
            inverse = 1.0 / pivot
            for b in range(a + 1, STEP):
                ratio = block[a][b] * inverse
                for c in range(b, STEP):
                    block[b][c] = block[b][c] - ratio * block[a][c]
                rows[b] = rows[b] - ratio * rows[a]
                cols[b] = cols[b] - ratio * cols[a]
            factor[j + a : j + a + 1] = rows[a] * (1.0 / jnp.sqrt(pivot))
            rows[a] = rows[a] * inverse
        for a in range(STEP):
            left = left - cols[a] * rows[a]
    inverse = factor[:, n:]
    out[...] = lax.dot_general(
        inverse,
        fresh[...].astype(F32),
        NN,
        precision=lax.Precision.HIGHEST,
        preferred_element_type=F32,
    ).astype(BF16)


def shift(value, axis, step, size):
    return lax.ppermute(value, axis, [(i, (i + step) % size) for i in range(size)])


def exchange(value, axes):
    return lax.all_to_all(value, axes, split_axis=0, concat_axis=0, tiled=True)


def body(x_start, weights, blocks, block_rows, block_cols, live_blocks):
    k, own = x_start.shape
    slots, tile, _ = blocks.shape
    ny, nx, nz = lax.axis_size("y"), lax.axis_size("x"), lax.axis_size(LINE)
    rows = 2 * ny * nx
    vertices = float(own * rows * nz)
    gains = weights.reshape(1, own)
    any_spec = pl.BlockSpec(memory_space=pl.ANY)
    any_in = pl.BlockSpec(memory_space=pltpu.HBM)
    places = jnp.concatenate([block_rows, block_cols, live_blocks])
    scaled = (x_start.astype(F32) * gains).astype(BF16)
    copies = jnp.broadcast_to(scaled[None], (nz, k, own))
    gram = None
    for sweep in range(2):
        with jax.named_scope("gather_line"):
            row_panel = exchange(copies, LINE)
        with jax.named_scope("gather_plane"):
            near_panel = lax.all_gather(scaled, ("y", "x"), axis=0)
        with jax.named_scope("gather_core"):
            other_panel = shift(near_panel, "core", 1, 2)
        with jax.named_scope("products"):
            plane_keep, plane_send, keep, send = call(
                products_kernel,
                [((ny * nx, k, own), BF16)] * 2 + [((nz // 2, k, own), BF16)] * 2,
                [SMEM] + [VMEM] * 3 + [any_in],
                [pltpu.VMEM((slots, tile, tile), BF16)]
                + [pltpu.VMEM((nz, k, own), F32), pltpu.VMEM((rows, k, own), F32)]
                + [pltpu.SemaphoreType.DMA((slots,))],
                4 * slots * k * tile * tile,
                blocks.size * 2,
                48,
            )(places, row_panel, near_panel, other_panel, blocks)
        with jax.named_scope("reduce_near"):
            got = shift(send, "near", 1, 2)
        with jax.named_scope("reduce_plane"):
            plane_got = shift(plane_send, "core", 1, 2)
            (plane,) = call(sum_kernel, [((ny * nx, k, own), BF16)], [VMEM] * 2)(
                plane_keep, plane_got
            )
            (from_plane,) = call(total_kernel, [((k, own), F32)], [VMEM])(
                exchange(plane, ("y", "x"))
            )
        with jax.named_scope("reduce_mid"):
            keep, send = call(
                halve_kernel, [((nz // 4, k, own), BF16)] * 2, [VMEM] * 2, flops=LONG
            )(keep, got)
            got = shift(send, "mid", 1, 2)
        with jax.named_scope("reduce_far"):
            got, from_plane = lax.optimization_barrier((got, from_plane))
            line = (keep.astype(F32) + got.astype(F32)).astype(BF16)
            from_line = exchange(line, "far")
        if sweep == 0:
            with jax.named_scope("between"):
                scaled, copies, gram = call(
                    between_kernel,
                    [((k, own), BF16), ((nz, k, own), BF16), ((k, k), F32)],
                    [VMEM] * 3,
                )(from_line, from_plane, gains)
        else:
            with jax.named_scope("last"):
                fresh, copies = call(
                    functools.partial(last_kernel, 1.0 / vertices),
                    [((k, own), BF16), ((rows, 1, 9 * 128), F32)],
                    [VMEM] * 4,
                )(from_line, from_plane, gains, gram)
    with jax.named_scope("gram_plane"):
        part = jnp.sum(exchange(copies, ROW), axis=0)
    with jax.named_scope("gram_line"):
        copies = jnp.broadcast_to(part[None], (nz,) + part.shape)
        part = jnp.sum(exchange(copies, LINE), axis=0)
    with jax.named_scope("gram_pair"):
        parts = lax.all_gather(part, "core", axis=0)
    with jax.named_scope("whiten"):
        (out,) = call(
            whiten_kernel,
            [((k, own), BF16)],
            [VMEM] * 2,
            [pltpu.VMEM((k, 2 * k), F32)],
        )(parts, fresh)
    return out


def solution(mesh):
    cells = ROW + LINE
    fine = Mesh(mesh.devices.reshape(4, 4, 2, 4, 2, 2), cells)
    return jax.shard_map(
        body,
        mesh=fine,
        in_specs=(P(None, cells), P(cells), P(cells, None, None), P(cells), P(cells), P(cells)),
        out_specs=P(None, cells),
        check_vma=False,
    )
```

```python
import functools

import jax
import jax.numpy as jnp
from jax import lax
from jax.experimental import pallas as pl
from jax.experimental.pallas import tpu as pltpu
from jax.sharding import Mesh, PartitionSpec as P

F32 = jnp.float32
BF16 = jnp.bfloat16
ROW = ("y", "x", "core")
LINE = ("far", "mid", "near")
RIDGE = 1e-06
STEP = 8
LONG = 1 << 44
VMEM = pl.BlockSpec(memory_space=pltpu.VMEM)
SMEM = pl.BlockSpec(memory_space=pltpu.SMEM)
MIB = 1024 * 1024
NT = (((1,), (1,)), ((), ()))
NN = (((1,), (0,)), ((), ()))


def call(kernel, outs, ins, scratch=(), flops=0, moved=0, room=16):
    return pl.pallas_call(
        kernel,
        out_shape=[jax.ShapeDtypeStruct(s, d) for s, d in outs],
        in_specs=ins,
        out_specs=[VMEM] * len(outs),
        scratch_shapes=list(scratch),
        compiler_params=pltpu.CompilerParams(vmem_limit_bytes=room * MIB),
        cost_estimate=pl.CostEstimate(flops=flops, bytes_accessed=moved, transcendentals=0),
    )


def products_kernel(
    places, row_panel, near_panel, other_panel, tiles, plane_keep, plane_send, keep, send,
    blocks, row_sum, col_sum, tile_sems,
):
    slots = tiles.shape[0]
    copies = [pltpu.make_async_copy(tiles.at[s], blocks.at[s], tile_sems.at[s]) for s in range(slots)]
    for s, copy in enumerate(copies):
        pl.when(s < places[2 * slots])(copy.start)
    row_sum[...] = jnp.zeros_like(row_sum)
    col_sum[...] = jnp.zeros_like(col_sum)
    half = row_panel.shape[2]
    first = lax.axis_index("core") == 0
    for s, copy in enumerate(copies):

        @pl.when(s < places[2 * slots])
        def _():
            copy.wait()
            r, c = places[s], places[slots + s]
            low, high = 2 * r, 2 * r + 1
            left, right = 2 * c, 2 * c + 1
            part = lax.dot_general(
                row_panel[low], blocks[s, :half, :], NN, preferred_element_type=F32
            ) + lax.dot_general(row_panel[high], blocks[s, half:, :], NN, preferred_element_type=F32)
            col_sum[left] += part[:, :half]
            col_sum[right] += part[:, half:]
            own, other = near_panel[c], other_panel[c]
            part = lax.dot_general(
                jnp.where(first, own, other), blocks[s, :, :half], NT, preferred_element_type=F32
            ) + lax.dot_general(
                jnp.where(first, other, own), blocks[s, :, half:], NT, preferred_element_type=F32
            )
            row_sum[low] += part[:, :half]
            row_sum[high] += part[:, half:]

    me = lax.axis_index("core")
    for chip in range(plane_keep.shape[0]):
        plane_keep[chip] = col_sum[2 * chip + me].astype(BF16)
        plane_send[chip] = col_sum[2 * chip + 1 - me].astype(BF16)
    me = lax.axis_index("near")
    for pair in range(keep.shape[0]):
        keep[pair] = row_sum[2 * pair + me].astype(BF16)
        send[pair] = row_sum[2 * pair + 1 - me].astype(BF16)


def sum_kernel(keep, got, out):
    out[...] = (keep[...].astype(F32) + got[...].astype(F32)).astype(BF16)


def total_kernel(pieces, out):
    sums = pieces[0].astype(F32)
    for k in range(1, pieces.shape[0]):
        sums += pieces[k].astype(F32)
    out[...] = sums


def halve_kernel(keep, got, stay, go):
    me = lax.axis_index("mid")
    for pair in range(stay.shape[0]):
        for out, at in ((stay, 2 * pair + me), (go, 2 * pair + 1 - me)):
            out[pair] = (keep[at].astype(F32) + got[at].astype(F32)).astype(BF16)


def spread(value, scaled, copies):
    scaled[...] = value
    for k in range(copies.shape[0]):
        copies[k] = value


def add_up(from_line, from_plane, weights):
    sums = from_plane[...]
    for k in range(from_line.shape[0]):
        sums += from_line[k].astype(F32)
    return sums * weights[...]


def between_kernel(from_line, from_plane, weights, scaled, copies, gram):
    fresh = add_up(from_line, from_plane, weights)
    spread((fresh * weights[...]).astype(BF16), scaled, copies)
    rounded = fresh.astype(BF16)
    gram[...] = lax.dot_general(rounded, rounded, NT, preferred_element_type=F32)


def masks(h):
    i = lax.broadcasted_iota(jnp.int32, (h, h), 0)
    j = lax.broadcasted_iota(jnp.int32, (h, h), 1)
    return (i >= j).astype(F32), (i == j).astype(F32)


def pack(gram):
    h = gram.shape[0] // 2
    lower, eye = masks(h)
    mixed = gram[:h, :h] * lower + gram[h:, h:] * (1.0 - lower)
    diagonal = jnp.sum(gram[h:, h:] * eye, axis=0, keepdims=True)
    lines = []
    for block in (mixed, gram[h:, :h]):
        wide = jnp.concatenate([block[8 * i : 8 * i + 8] for i in range(h // 8)], axis=1)
        lines += [wide[i : i + 1] for i in range(8)]
    lines.append(jnp.concatenate([diagonal] * (128 // h), axis=1))
    lines.append(jnp.zeros_like(lines[-1]))
    return jnp.concatenate(lines, axis=1)


def unpack(row, n):
    h = n // 2
    lower, eye = masks(h)
    blocks = []
    for b in range(2):
        at = [row[:, 128 * (8 * b + i) : 128 * (8 * b + i + 1)] for i in range(8)]
        wide = jnp.concatenate(at, axis=0)
        blocks.append(jnp.concatenate([wide[:, h * i : h * i + h] for i in range(h // 8)], axis=0))
    mixed, corner = blocks
    diagonal = row[:, 2048 : 2048 + h] * eye
    upper = mixed * (1.0 - lower)
    strict = mixed * (lower - eye)
    first = strict + strict.T + mixed * eye
    second = upper + upper.T + diagonal
    return jnp.concatenate(
        [jnp.concatenate([first, corner.T], axis=1), jnp.concatenate([corner, second], axis=1)],
        axis=0,
    )


def last_kernel(scale, from_line, from_plane, weights, first, fresh, copies):
    rounded = add_up(from_line, from_plane, weights).astype(BF16)
    fresh[...] = rounded
    gram = lax.dot_general(rounded, rounded, NT, preferred_element_type=F32)
    packed = pack((gram + RIDGE * first[...]) * scale)
    h = packed.shape[1] // 2
    for k in range(copies.shape[0]):
        copies[k] = packed[:, h:] if k % 2 else packed[:, :h]


def whiten_kernel(parts, fresh, out, factor):
    packed = jnp.concatenate([parts[0], parts[1]], axis=1)
    n = fresh.shape[0]
    matrix = unpack(packed, n)
    eye = masks(n)[1]
    left = jnp.concatenate([matrix + RIDGE * RIDGE * eye, eye], axis=1)
    base = 0
    for j in range(0, n, STEP):
        if j - base == 8:
            left = left[8:]
            base = j
        i = j - base
        wide = (left.shape[0], 2 * n)
        cols = [jnp.broadcast_to(left[:, j + a : j + a + 1], wide) for a in range(STEP)]
        rows = [left[i + a : i + a + 1] for a in range(STEP)]
        block = [[cols[b][i + a : i + a + 1] for b in range(STEP)] for a in range(STEP)]
        for a in range(STEP):
            pivot = block[a][a]
            inverse = 1.0 / pivot
            for b in range(a + 1, STEP):
                ratio = block[a][b] * inverse
                for c in range(b, STEP):
                    block[b][c] = block[b][c] - ratio * block[a][c]
                rows[b] = rows[b] - ratio * rows[a]
                cols[b] = cols[b] - ratio * cols[a]
            factor[j + a : j + a + 1] = rows[a] * (1.0 / jnp.sqrt(pivot))
            rows[a] = rows[a] * inverse
        for a in range(STEP):
            left = left - cols[a] * rows[a]
    inverse = factor[:, n:]
    out[...] = lax.dot_general(
        inverse,
        fresh[...].astype(F32),
        NN,
        precision=lax.Precision.HIGHEST,
        preferred_element_type=F32,
    ).astype(BF16)


def shift(value, axis, step, size):
    return lax.ppermute(value, axis, [(i, (i + step) % size) for i in range(size)])


def exchange(value, axes):
    return lax.all_to_all(value, axes, split_axis=0, concat_axis=0, tiled=True)


def body(x_start, weights, blocks, block_rows, block_cols, live_blocks):
    k, own = x_start.shape
    slots, tile, _ = blocks.shape
    ny, nx, nz = lax.axis_size("y"), lax.axis_size("x"), lax.axis_size(LINE)
    rows = 2 * ny * nx
    vertices = float(own * rows * nz)
    gains = weights.reshape(1, own)
    any_spec = pl.BlockSpec(memory_space=pl.ANY)
    any_in = pl.BlockSpec(memory_space=pltpu.HBM)
    scaled = (x_start.astype(F32) * gains).astype(BF16)
    copies = jnp.broadcast_to(scaled[None], (nz, k, own))
    gram = None
    for sweep in range(2):
        with jax.named_scope("gather_line"):
            row_panel = exchange(copies, LINE)
        with jax.named_scope("gather_plane"):
            near_panel = lax.all_gather(scaled, ("y", "x"), axis=0)
        with jax.named_scope("gather_core"):
            other_panel = shift(near_panel, "core", 1, 2)
        with jax.named_scope("places"):
            tile_rows, near_panel = lax.optimization_barrier((block_rows, near_panel))
            places = jnp.concatenate([tile_rows, block_cols, live_blocks])
        with jax.named_scope("products"):
            plane_keep, plane_send, keep, send = call(
                products_kernel,
                [((ny * nx, k, own), BF16)] * 2 + [((nz // 2, k, own), BF16)] * 2,
                [SMEM] + [VMEM] * 3 + [any_in],
                [pltpu.VMEM((slots, tile, tile), BF16)]
                + [pltpu.VMEM((nz, k, own), F32), pltpu.VMEM((rows, k, own), F32)]
                + [pltpu.SemaphoreType.DMA((slots,))],
                4 * slots * k * tile * tile,
                blocks.size * 2,
                48,
            )(places, row_panel, near_panel, other_panel, blocks)
        with jax.named_scope("reduce_near"):
            got = shift(send, "near", 1, 2)
        with jax.named_scope("reduce_plane"):
            plane_got = shift(plane_send, "core", 1, 2)
            (plane,) = call(sum_kernel, [((ny * nx, k, own), BF16)], [VMEM] * 2)(
                plane_keep, plane_got
            )
            (from_plane,) = call(total_kernel, [((k, own), F32)], [VMEM])(
                exchange(plane, ("y", "x"))
            )
        with jax.named_scope("reduce_mid"):
            keep, send = call(
                halve_kernel, [((nz // 4, k, own), BF16)] * 2, [VMEM] * 2, flops=LONG
            )(keep, got)
            got = shift(send, "mid", 1, 2)
        with jax.named_scope("reduce_far"):
            got, from_plane = lax.optimization_barrier((got, from_plane))
            line = (keep.astype(F32) + got.astype(F32)).astype(BF16)
            from_line = exchange(line, "far")
        if sweep == 0:
            with jax.named_scope("between"):
                scaled, copies, gram = call(
                    between_kernel,
                    [((k, own), BF16), ((nz, k, own), BF16), ((k, k), F32)],
                    [VMEM] * 3,
                )(from_line, from_plane, gains)
        else:
            with jax.named_scope("last"):
                fresh, copies = call(
                    functools.partial(last_kernel, 1.0 / vertices),
                    [((k, own), BF16), ((rows, 1, 9 * 128), F32)],
                    [VMEM] * 4,
                )(from_line, from_plane, gains, gram)
    with jax.named_scope("gram_plane"):
        part = jnp.sum(exchange(copies, ROW), axis=0)
    with jax.named_scope("gram_line"):
        copies = jnp.broadcast_to(part[None], (nz,) + part.shape)
        part = jnp.sum(exchange(copies, LINE), axis=0)
    with jax.named_scope("gram_pair"):
        parts = lax.all_gather(part, "core", axis=0)
    with jax.named_scope("whiten"):
        (out,) = call(
            whiten_kernel,
            [((k, own), BF16)],
            [VMEM] * 2,
            [pltpu.VMEM((k, 2 * k), F32)],
        )(parts, fresh)
    return out


def solution(mesh):
    cells = ROW + LINE
    fine = Mesh(mesh.devices.reshape(4, 4, 2, 4, 2, 2), cells)
    return jax.shard_map(
        body,
        mesh=fine,
        in_specs=(P(None, cells), P(cells), P(cells, None, None), P(cells), P(cells), P(cells)),
        out_specs=P(None, cells),
        check_vma=False,
    )
```

```python
import functools

import jax
import jax.numpy as jnp
from jax import lax
from jax.experimental import pallas as pl
from jax.experimental.pallas import tpu as pltpu
from jax.sharding import Mesh, PartitionSpec as P

F32 = jnp.float32
BF16 = jnp.bfloat16
ROW = ("y", "x", "core")
LINE = ("far", "mid", "near")
RIDGE = 1e-06
STEP = 8
GROUP = 3
LONG = 1 << 44
VMEM = pl.BlockSpec(memory_space=pltpu.VMEM)
SMEM = pl.BlockSpec(memory_space=pltpu.SMEM)
MIB = 1024 * 1024
NT = (((1,), (1,)), ((), ()))
NN = (((1,), (0,)), ((), ()))


def call(kernel, outs, ins, scratch=(), flops=0, moved=0, room=16):
    return pl.pallas_call(
        kernel,
        out_shape=[jax.ShapeDtypeStruct(s, d) for s, d in outs],
        in_specs=ins,
        out_specs=[VMEM] * len(outs),
        scratch_shapes=list(scratch),
        compiler_params=pltpu.CompilerParams(vmem_limit_bytes=room * MIB),
        cost_estimate=pl.CostEstimate(flops=flops, bytes_accessed=moved, transcendentals=0),
    )


def products_kernel(
    places, row_panel, near_panel, other_panel, tiles, plane_keep, plane_send, keep, send,
    blocks, row_sum, col_sum, tile_sems,
):
    slots = tiles.shape[0]
    copies = [pltpu.make_async_copy(tiles.at[s], blocks.at[s], tile_sems.at[s]) for s in range(slots)]
    live = places[2 * slots]
    for s, copy in enumerate(copies):
        pl.when(s - s % GROUP < live)(copy.start)
    row_sum[...] = jnp.zeros_like(row_sum)
    col_sum[...] = jnp.zeros_like(col_sum)
    half = row_panel.shape[2]
    first_core = lax.axis_index("core") == 0
    row_spare, col_spare = row_panel.shape[0], 2 * near_panel.shape[0]
    for start in range(0, slots, GROUP):

        @pl.when(start < live)
        def _():
            group = range(start, min(start + GROUP, slots))
            for s in group:
                copies[s].wait()
            terms = []
            for s in group:
                r, c = places[s], places[slots + s]
                low, high = 2 * r, 2 * r + 1
                down = lax.dot_general(
                    row_panel[low], blocks[s, :half, :], NN, preferred_element_type=F32
                ) + lax.dot_general(
                    row_panel[high], blocks[s, half:, :], NN, preferred_element_type=F32
                )
                own, other = near_panel[c], other_panel[c]
                across = lax.dot_general(
                    jnp.where(first_core, own, other),
                    blocks[s, :, :half],
                    NT,
                    preferred_element_type=F32,
                ) + lax.dot_general(
                    jnp.where(first_core, other, own),
                    blocks[s, :, half:],
                    NT,
                    preferred_element_type=F32,
                )
                rows = [jnp.where(s < live, at, row_spare) for at in (low, high)]
                cols = [jnp.where(s < live, at, col_spare) for at in (2 * c, 2 * c + 1)]
                terms.append((rows, cols, down, across))
            for rows, cols, down, across in terms:
                col_sum[cols[0]] += down[:, :half]
                col_sum[cols[1]] += down[:, half:]
                row_sum[rows[0]] += across[:, :half]
                row_sum[rows[1]] += across[:, half:]

    me = lax.axis_index("core")
    for chip in range(plane_keep.shape[0]):
        plane_keep[chip] = col_sum[2 * chip + me].astype(BF16)
        plane_send[chip] = col_sum[2 * chip + 1 - me].astype(BF16)
    me = lax.axis_index("near")
    for pair in range(keep.shape[0]):
        keep[pair] = row_sum[2 * pair + me].astype(BF16)
        send[pair] = row_sum[2 * pair + 1 - me].astype(BF16)


def sum_kernel(keep, got, out):
    out[...] = (keep[...].astype(F32) + got[...].astype(F32)).astype(BF16)


def total_kernel(pieces, out):
    sums = pieces[0].astype(F32)
    for k in range(1, pieces.shape[0]):
        sums += pieces[k].astype(F32)
    out[...] = sums


def halve_kernel(keep, got, stay, go):
    me = lax.axis_index("mid")
    for pair in range(stay.shape[0]):
        for out, at in ((stay, 2 * pair + me), (go, 2 * pair + 1 - me)):
            out[pair] = (keep[at].astype(F32) + got[at].astype(F32)).astype(BF16)


def spread(value, scaled, copies):
    scaled[...] = value
    for k in range(copies.shape[0]):
        copies[k] = value


def add_up(from_line, from_plane, weights):
    sums = from_plane[...]
    for k in range(from_line.shape[0]):
        sums += from_line[k].astype(F32)
    return sums * weights[...]


def between_kernel(from_line, from_plane, weights, scaled, copies, gram):
    fresh = add_up(from_line, from_plane, weights)
    spread((fresh * weights[...]).astype(BF16), scaled, copies)
    rounded = fresh.astype(BF16)
    gram[...] = lax.dot_general(rounded, rounded, NT, preferred_element_type=F32)


def masks(h):
    i = lax.broadcasted_iota(jnp.int32, (h, h), 0)
    j = lax.broadcasted_iota(jnp.int32, (h, h), 1)
    return (i >= j).astype(F32), (i == j).astype(F32)


def pack(gram):
    h = gram.shape[0] // 2
    lower, eye = masks(h)
    mixed = gram[:h, :h] * lower + gram[h:, h:] * (1.0 - lower)
    diagonal = jnp.sum(gram[h:, h:] * eye, axis=0, keepdims=True)
    lines = []
    for block in (mixed, gram[h:, :h]):
        wide = jnp.concatenate([block[8 * i : 8 * i + 8] for i in range(h // 8)], axis=1)
        lines += [wide[i : i + 1] for i in range(8)]
    lines.append(jnp.concatenate([diagonal] * (128 // h), axis=1))
    lines.append(jnp.zeros_like(lines[-1]))
    return jnp.concatenate(lines, axis=1)


def unpack(row, n):
    h = n // 2
    lower, eye = masks(h)
    blocks = []
    for b in range(2):
        at = [row[:, 128 * (8 * b + i) : 128 * (8 * b + i + 1)] for i in range(8)]
        wide = jnp.concatenate(at, axis=0)
        blocks.append(jnp.concatenate([wide[:, h * i : h * i + h] for i in range(h // 8)], axis=0))
    mixed, corner = blocks
    diagonal = row[:, 2048 : 2048 + h] * eye
    upper = mixed * (1.0 - lower)
    strict = mixed * (lower - eye)
    first = strict + strict.T + mixed * eye
    second = upper + upper.T + diagonal
    return jnp.concatenate(
        [jnp.concatenate([first, corner.T], axis=1), jnp.concatenate([corner, second], axis=1)],
        axis=0,
    )


def last_kernel(scale, from_line, from_plane, weights, first, fresh, copies):
    rounded = add_up(from_line, from_plane, weights).astype(BF16)
    fresh[...] = rounded
    gram = lax.dot_general(rounded, rounded, NT, preferred_element_type=F32)
    packed = pack((gram + RIDGE * first[...]) * scale)
    h = packed.shape[1] // 2
    for k in range(copies.shape[0]):
        copies[k] = packed[:, h:] if k % 2 else packed[:, :h]


def whiten_kernel(parts, fresh, out, factor):
    packed = jnp.concatenate([parts[0], parts[1]], axis=1)
    n = fresh.shape[0]
    matrix = unpack(packed, n)
    eye = masks(n)[1]
    left = jnp.concatenate([matrix + RIDGE * RIDGE * eye, eye], axis=1)
    base = 0
    for j in range(0, n, STEP):
        if j - base == 8:
            left = left[8:]
            base = j
        i = j - base
        wide = (left.shape[0], 2 * n)
        cols = [jnp.broadcast_to(left[:, j + a : j + a + 1], wide) for a in range(STEP)]
        rows = [left[i + a : i + a + 1] for a in range(STEP)]
        block = [[cols[b][i + a : i + a + 1] for b in range(STEP)] for a in range(STEP)]
        for a in range(STEP):
            pivot = block[a][a]
            inverse = 1.0 / pivot
            for b in range(a + 1, STEP):
                ratio = block[a][b] * inverse
                for c in range(b, STEP):
                    block[b][c] = block[b][c] - ratio * block[a][c]
                rows[b] = rows[b] - ratio * rows[a]
                cols[b] = cols[b] - ratio * cols[a]
            factor[j + a : j + a + 1] = rows[a] * (1.0 / jnp.sqrt(pivot))
            rows[a] = rows[a] * inverse
        for a in range(STEP):
            left = left - cols[a] * rows[a]
    inverse = factor[:, n:]
    out[...] = lax.dot_general(
        inverse,
        fresh[...].astype(F32),
        NN,
        precision=lax.Precision.HIGHEST,
        preferred_element_type=F32,
    ).astype(BF16)


def shift(value, axis, step, size):
    return lax.ppermute(value, axis, [(i, (i + step) % size) for i in range(size)])


def exchange(value, axes):
    return lax.all_to_all(value, axes, split_axis=0, concat_axis=0, tiled=True)


def body(x_start, weights, blocks, block_rows, block_cols, live_blocks):
    k, own = x_start.shape
    slots, tile, _ = blocks.shape
    ny, nx, nz = lax.axis_size("y"), lax.axis_size("x"), lax.axis_size(LINE)
    rows = 2 * ny * nx
    vertices = float(own * rows * nz)
    gains = weights.reshape(1, own)
    any_spec = pl.BlockSpec(memory_space=pl.ANY)
    any_in = pl.BlockSpec(memory_space=pltpu.HBM)
    scaled = (x_start.astype(F32) * gains).astype(BF16)
    copies = jnp.broadcast_to(scaled[None], (nz, k, own))
    gram = None
    for sweep in range(2):
        with jax.named_scope("gather_line"):
            row_panel = exchange(copies, LINE)
        with jax.named_scope("gather_plane"):
            near_panel = lax.all_gather(scaled, ("y", "x"), axis=0)
        with jax.named_scope("gather_core"):
            other_panel = shift(near_panel, "core", 1, 2)
        with jax.named_scope("places"):
            tile_rows, near_panel = lax.optimization_barrier((block_rows, near_panel))
            places = jnp.concatenate([tile_rows, block_cols, live_blocks])
        with jax.named_scope("products"):
            plane_keep, plane_send, keep, send = call(
                products_kernel,
                [((ny * nx, k, own), BF16)] * 2 + [((nz // 2, k, own), BF16)] * 2,
                [SMEM] + [VMEM] * 3 + [any_in],
                [pltpu.VMEM((slots, tile, tile), BF16)]
                + [pltpu.VMEM((nz + 1, k, own), F32), pltpu.VMEM((rows + 1, k, own), F32)]
                + [pltpu.SemaphoreType.DMA((slots,))],
                4 * slots * k * tile * tile,
                blocks.size * 2,
                48,
            )(places, row_panel, near_panel, other_panel, blocks)
        with jax.named_scope("reduce_near"):
            got = shift(send, "near", 1, 2)
        with jax.named_scope("reduce_plane"):
            plane_got = shift(plane_send, "core", 1, 2)
            (plane,) = call(sum_kernel, [((ny * nx, k, own), BF16)], [VMEM] * 2)(
                plane_keep, plane_got
            )
            (from_plane,) = call(total_kernel, [((k, own), F32)], [VMEM])(
                exchange(plane, ("y", "x"))
            )
        with jax.named_scope("reduce_mid"):
            keep, send = call(
                halve_kernel, [((nz // 4, k, own), BF16)] * 2, [VMEM] * 2, flops=LONG
            )(keep, got)
            got = shift(send, "mid", 1, 2)
        with jax.named_scope("reduce_far"):
            got, from_plane = lax.optimization_barrier((got, from_plane))
            line = (keep.astype(F32) + got.astype(F32)).astype(BF16)
            from_line = exchange(line, "far")
        if sweep == 0:
            with jax.named_scope("between"):
                scaled, copies, gram = call(
                    between_kernel,
                    [((k, own), BF16), ((nz, k, own), BF16), ((k, k), F32)],
                    [VMEM] * 3,
                )(from_line, from_plane, gains)
        else:
            with jax.named_scope("last"):
                fresh, copies = call(
                    functools.partial(last_kernel, 1.0 / vertices),
                    [((k, own), BF16), ((rows, 1, 9 * 128), F32)],
                    [VMEM] * 4,
                )(from_line, from_plane, gains, gram)
    with jax.named_scope("gram_plane"):
        part = jnp.sum(exchange(copies, ROW), axis=0)
    with jax.named_scope("gram_line"):
        copies = jnp.broadcast_to(part[None], (nz,) + part.shape)
        part = jnp.sum(exchange(copies, LINE), axis=0)
    with jax.named_scope("gram_pair"):
        parts = lax.all_gather(part, "core", axis=0)
    with jax.named_scope("whiten"):
        (out,) = call(
            whiten_kernel,
            [((k, own), BF16)],
            [VMEM] * 2,
            [pltpu.VMEM((k, 2 * k), F32)],
        )(parts, fresh)
    return out


def solution(mesh):
    cells = ROW + LINE
    fine = Mesh(mesh.devices.reshape(4, 4, 2, 4, 2, 2), cells)
    return jax.shard_map(
        body,
        mesh=fine,
        in_specs=(P(None, cells), P(cells), P(cells, None, None), P(cells), P(cells), P(cells)),
        out_specs=P(None, cells),
        check_vma=False,
    )
```
